512 devices in a mesh: gx: 8 (over z_lo), gy: 8 (over x, z_hi), gz: 8 (over y, core).
Axes of the slice: x: 4, y: 4, z: 16 (z_hi: 2, z_lo: 8; z = z_hi * 8 + z_lo), core: 2. Of those that a mesh axis runs over, the one named last changes fastest.
Arguments:
- inputs: bfloat16 [2048, 12288], P('gx', 'gz'), may hold values from -6 to 6
- weight: bfloat16 [12288, 24576], P(('gz', 'gx'), 'gy'), may hold values from -0.0546875 to 0.0546875
- grad_out: bfloat16 [2048, 24576], P(('gx', 'gz'), 'gy'), may hold values from -6 to 6
- pre_act: bfloat16 [2048, 24576], P(('gx', 'gz'), 'gy'), may hold values from -6 to 6
Outputs:
- grad_in: bfloat16 [2048, 12288], P('gx', 'gz')
- grad_weight: bfloat16 [12288, 24576], P(('gz', 'gx'), 'gy')
The draws below stay inside these ranges and needn't reach their ends.
All inputs are finite; a program needn't handle non-finite values.
Results may differ from the reference program's by a relative error of at most 0.0049.
Values may be sent and summed in bfloat16 or wider, within the bound.
No kernel may reach another device: no remote copies, remote signals or barrier semaphores. Data moves between devices by JAX's collectives and lax.ppermute only.
A program may use at most 64 MiB of HBM per device.

```python
import jax
import jax.numpy as jnp

D = 12288
FF = 24576
TOKENS = 2048


def level_of(rng, shape, split, smallest, high):
    factor_of = 1.0
    for dim, blocks in split:
        draws = jax.random.uniform(jax.random.fold_in(jax.random.fold_in(rng, 6), dim), (blocks,), jnp.float32, smallest / len(split), high / len(split))
        factor_of = factor_of * jnp.repeat(jnp.exp(draws), shape[dim] // blocks).reshape((-1,) + (1,) * (len(shape) - 1 - dim))
    return factor_of


def normal_values(key, shape, spread, limit, split=(), held_as=jnp.bfloat16):
    loudness = level_of(key, shape, split, -0.22, 0.18) if split else 1.0
    entries = jax.random.normal(key, shape, jnp.float32) * spread * loudness
    return jnp.minimum(jnp.maximum(entries, -limit), limit).astype(held_as)


def setup_inputs(seed: int = 0) -> dict:
    keys = jax.random.split(jax.random.key(seed), 5)
    inputs = normal_values(keys[0], (TOKENS, D), 1.0, 6.0, ((0, 8), (1, 8)))
    weight = normal_values(keys[1], (D, FF), D ** -0.5, 0.0546875, ((0, 64), (1, 8)))
    grad_out = normal_values(keys[2], (TOKENS, FF), 1.0, 6.0, ((0, 64), (1, 8)))
    pre_act = normal_values(keys[3], (TOKENS, FF), 1.0, 6.0, ((0, 64), (1, 8)))
    return {"inputs": inputs, "weight": weight, "grad_out": grad_out, "pre_act": pre_act}


def gelu_slope(value):
    scale = 0.7978845608028654
    tangent = jnp.tanh(scale * (value + 0.044715 * value * value * value))
    inner = scale * (1.0 + 3.0 * 0.044715 * value * value)
    return 0.5 * (1.0 + tangent) + 0.5 * value * (1.0 - tangent * tangent) * inner


def reference(inputs, weight, grad_out, pre_act):
    grad_hidden = (grad_out.astype(jnp.float32) * gelu_slope(pre_act.astype(jnp.float32))).astype(jnp.bfloat16)
    grad_in = jnp.dot(grad_hidden, weight.T, preferred_element_type=jnp.float32).astype(jnp.bfloat16)
    grad_weight = jnp.dot(inputs.T, grad_hidden, preferred_element_type=jnp.float32).astype(jnp.bfloat16)
    return grad_in, grad_weight
```

```python
import jax
import jax.numpy as jnp
from jax import lax
from jax.sharding import Mesh
from jax.sharding import PartitionSpec as P

RING = (0, 2, 4, 6, 7, 5, 3, 1)
PLACE = tuple(RING.index(k) for k in range(8))
F32 = jnp.float32
BF16 = jnp.bfloat16


def gelu_slope(value):
    scale = 0.7978845608028654
    tangent = jnp.tanh(scale * (value + 0.044715 * value * value * value))
    inner = scale * (1.0 + 3.0 * 0.044715 * value * value)
    return 0.5 * (1.0 + tangent) + 0.5 * value * (1.0 - tangent * tangent) * inner


def hop(value, step):
    return lax.ppermute(value, "gx", [(RING[q], RING[(q + step) % 8]) for q in range(8)])


def swap(value):
    return lax.ppermute(value, "core", [(0, 1), (1, 0)])


def shards(inputs, weight, grad_out, pre_act):
    core = lax.axis_index("core")
    place = jnp.asarray(PLACE, jnp.int32)[lax.axis_index("gx")]
    gh = (grad_out.astype(F32) * gelu_slope(pre_act.astype(F32))).astype(BF16)
    other_weight = swap(weight)

    part = lax.dynamic_slice(inputs, (lax.axis_index("x") * 64, 0), (64, 1536))
    part = part.reshape(2, 32, 8, 192).transpose(2, 0, 1, 3).reshape(512, 192)
    part = lax.all_to_all(part, ("gx", "core"), split_axis=0, concat_axis=0, tiled=True)
    cols = lax.all_gather(part.reshape(8, 2, 32, 192), "x", axis=0)
    cols = jnp.where(core == 0, cols, cols[:, :, ::-1])
    cols = jnp.stack([cols[:, k] for k in RING], 0)
    cols = lax.dynamic_slice_in_dim(jnp.concatenate([cols, cols], 0), (place + 4) % 8, 8, 0)
    cols = cols.transpose(0, 1, 3, 2, 4)

    up, down = [gh], [gh]
    for _ in range(3):
        up.append(hop(up[-1], 1))
        down.append(hop(down[-1], -1))
    last = jnp.concatenate([hop(up[3][:16], 1), hop(down[3][16:], -1)], 0)
    groups = [([4], gh[None])]
    groups += [([4 - s, 4 + s], jnp.stack([up[s], down[s]], 0)) for s in (1, 2, 3)]
    groups += [([0], last[None])]
    blocks = [None] * 8
    weight_sum = 0.0
    for places, value in groups:
        n = len(places)
        full = lax.all_gather(value, "y", axis=0)
        flat = full.reshape(128 * n, 3072)
        mine = jnp.stack([cols[p] for p in places], 1).reshape(128 * n, 384)
        weight_sum = weight_sum + lax.dot_general(
            mine, flat, (((0,), (0,)), ((), ())), preferred_element_type=F32
        )
        halves = [
            lax.dot_general(flat, w, (((1,), (1,)), ((), ())), preferred_element_type=F32)
            .astype(BF16)
            .reshape(4, n, 32, 192)
            for w in (weight, other_weight)
        ]
        for i, p in enumerate(places):
            blocks[p] = jnp.stack([h[:, i] for h in halves], 1)

    rows = jnp.stack(blocks, 0)
    rows = lax.dynamic_slice_in_dim(jnp.concatenate([rows, rows], 0), (12 - place) % 8, 8, 0)
    rows = jnp.where(core == 0, rows, rows[:, :, ::-1])
    rows = jnp.stack([rows[q] for q in PLACE], 1)
    rows = lax.all_to_all(rows, "x", split_axis=0, concat_axis=0, tiled=True)
    rows = jnp.sum(rows.astype(F32), 0).astype(BF16)
    rows = jnp.stack([rows, rows], 1).reshape(32, 32, 192)
    rows = lax.all_to_all(rows, ("gx", "zh", "core"), split_axis=0, concat_axis=0, tiled=True)
    rows = jnp.sum(rows.reshape(8, 2, 2, 32, 192).astype(F32), 1).astype(BF16)
    rows = rows.transpose(1, 2, 0, 3).reshape(64, 1536)
    grad_in = lax.all_gather(rows, "x", axis=0, tiled=True)

    grad_weight = (weight_sum[:192] + swap(weight_sum[192:])).astype(BF16)
    return grad_in, grad_weight


def solution(mesh):
    fine = Mesh(mesh.devices.reshape(8, 4, 2, 4, 2), ("gx", "x", "zh", "y", "core"))
    split = P(("gx", "y", "core"), ("x", "zh"))
    tokens = P("gx", ("y", "core"))
    rows = P(("y", "core", "gx"), ("x", "zh"))
    return jax.shard_map(
        shards,
        mesh=fine,
        in_specs=(tokens, rows, split, split),
        out_specs=(tokens, rows),
        check_vma=False,
    )
```

```python
import jax
import jax.numpy as jnp
from jax import lax
from jax.experimental import pallas as pl
from jax.experimental.pallas import tpu as pltpu
from jax.sharding import Mesh
from jax.sharding import PartitionSpec as P

RING = (0, 2, 4, 6, 7, 5, 3, 1)
PLACE = tuple(RING.index(k) for k in range(8))
STEPS = (0, -1, 1, -2, 2, -3, 3, 4)
F32 = jnp.float32
BF16 = jnp.bfloat16
SMEM = pl.BlockSpec(memory_space=pltpu.SMEM)
VMEM = pl.BlockSpec(memory_space=pltpu.VMEM)
LIMIT = pltpu.CompilerParams(vmem_limit_bytes=48 * 1024 * 1024)


def gelu_slope(value):
    scale = 0.7978845608028654
    tangent = jnp.tanh(scale * (value + 0.044715 * value * value * value))
    inner = scale * (1.0 + 3.0 * 0.044715 * value * value)
    return 0.5 * (1.0 + tangent) + 0.5 * value * (1.0 - tangent * tangent) * inner


def hop(value, step):
    return lax.ppermute(value, "gx", [(RING[q], RING[(q + step) % 8]) for q in range(8)])


def swap(value, axis):
    return lax.ppermute(value, axis, [(0, 1), (1, 0)])


def across(value):
    return lax.ppermute(value, ("yp", "yl"), [(k, 3 - k) for k in range(4)])


def product_kernel(owner, dest, *refs):
    pieces, weights, (rows, whole) = refs[:12], refs[12:16], refs[16:]
    at = 0
    for piece in pieces:
        whole[at : at + piece.shape[0]] = piece[...]
        at += piece.shape[0]
    for j, weight in enumerate(weights):
        block = lax.dot_general(
            whole[...], weight[...], (((1,), (1,)), ((), ())), preferred_element_type=F32
        ).astype(BF16)
        for side in range(2):
            for slot in range(8):
                for half in range(2):
                    first = side * 256 + slot * 32 + half * 16
                    rows[side * 2 + half, dest[j], owner[slot]] = block[first : first + 16]


def weight_kernel(owner, dest, cols, whole, keep, send, turned):
    @pl.when(pl.program_id(0) == 0)
    def _():
        for j in range(4):
            parts = [
                cols[side * 2 + half, owner[slot], dest[j]]
                for side in range(2)
                for slot in range(8)
                for half in range(2)
            ]
            turned[j * 192 : (j + 1) * 192] = jnp.concatenate(parts, 0).T

    total = jnp.dot(turned[...], whole[...], preferred_element_type=F32)
    for j in range(2):
        keep[j] = total[j * 192 : (j + 1) * 192]
        send[j] = total[384 + j * 192 : 384 + (j + 1) * 192]


def add_kernel(parts, out):
    for k in range(8):
        for j in range(4):
            total = parts[0, j, k].astype(F32)
            for i in range(1, 4):
                total = total + parts[i, j, k].astype(F32)
            total = total.astype(BF16)
            out[k, 0, j] = total
            out[k, 1, j] = total


def pair_kernel(parts, out):
    sums = [parts[k, 0].astype(F32) + parts[k, 1].astype(F32) for k in range(8)]
    out[...] = jnp.concatenate(sums, 1).astype(BF16)


def place_kernel(which, parts, out):
    mine = which[0]
    for p in range(2):
        side = jnp.where(mine == p, 0, 1)
        for s in range(2):
            source = jnp.where(mine == p, s, 1 - s)
            for c in range(2):
                for half in range(2):
                    first = p * 128 + s * 64 + c * 32 + half * 16
                    out[first : first + 16] = parts[side * 2 + half, source * 2 + c]


def shards(inputs, weight, grad_out, pre_act):
    x, yp, yl, core = (lax.axis_index(a) for a in ("x", "yp", "yl", "core"))
    place = jnp.asarray(PLACE, jnp.int32)[lax.axis_index("gx")]
    owner = jnp.asarray(RING, jnp.int32)[(place + jnp.asarray(STEPS, jnp.int32)) % 8]
    dest = jnp.stack([a * 2 + b for b in (core, 1 - core) for a in (yl, 1 - yl)]).astype(jnp.int32)

    gh = (grad_out.astype(F32) * gelu_slope(pre_act.astype(F32))).astype(BF16)

    beside = swap(weight, "yl")
    weights = (weight, beside, swap(weight, "core"), swap(beside, "core"))

    up, down = [gh], [gh]
    for _ in range(3):
        up.append(hop(up[-1], 1))
        down.append(hop(down[-1], -1))
    last = [hop(up[3][:16], 1), hop(down[3][16:], -1)]
    own = [gh, up[1], down[1], up[2], down[2], up[3], down[3], *last]
    far = [across(jnp.concatenate(v, 0)) for v in (own[:5], own[5:7], last)]

    part = lax.dynamic_slice(inputs, (jnp.where(x < 2, yp, 1 - yp) * 128, 0), (128, 1536))
    part = part.reshape(2, 2, 2, 16, 8, 192)
    part = jnp.where(x % 2 == 0, part[:, :, 0], part[:, :, 1])
    part = jnp.where(x < 2, part, part[::-1])
    part = part.transpose(3, 0, 1, 2, 4).reshape(32, 16, 192)
    part = lax.all_to_all(part, ("gx", "yl", "core"), split_axis=0, concat_axis=0, tiled=True)
    cols = lax.all_gather(part.reshape(8, 4, 16, 192), "x", axis=0)

    rows, whole = pl.pallas_call(
        product_kernel,
        out_shape=(
            jax.ShapeDtypeStruct((4, 4, 8, 16, 192), BF16),
            jax.ShapeDtypeStruct((512, 3072), BF16),
        ),
        in_specs=[SMEM, SMEM] + [VMEM] * 16,
        out_specs=(VMEM, VMEM),
        compiler_params=LIMIT,
        cost_estimate=pl.CostEstimate(
            flops=2 * 512 * 3072 * 768, bytes_accessed=12 << 20, transcendentals=0
        ),
        name="products",
    )(owner, dest, *own, *far, *weights)

    rows = lax.all_to_all(
        rows.reshape(16, 8, 16, 192), ("x", "yl", "core"), split_axis=0, concat_axis=0, tiled=True
    )
    rows = pl.pallas_call(
        add_kernel,
        out_shape=jax.ShapeDtypeStruct((8, 2, 4, 16, 192), BF16),
        in_specs=[VMEM],
        out_specs=VMEM,
        compiler_params=LIMIT,
        name="sum_x",
    )(rows.reshape(4, 4, 8, 16, 192))
    rows = lax.all_to_all(
        rows.reshape(16, 64, 192), ("gx", "zh"), split_axis=0, concat_axis=0, tiled=True
    )
    rows = pl.pallas_call(
        pair_kernel,
        out_shape=jax.ShapeDtypeStruct((64, 1536), BF16),
        in_specs=[VMEM],
        out_specs=VMEM,
        compiler_params=LIMIT,
        name="sum_z",
    )(rows.reshape(8, 2, 64, 192))
    rows = lax.all_gather(rows, "x", axis=0)
    grad_in = pl.pallas_call(
        place_kernel,
        out_shape=jax.ShapeDtypeStruct((256, 1536), BF16),
        in_specs=[SMEM, VMEM],
        out_specs=VMEM,
        compiler_params=LIMIT,
        name="place",
    )(yp.astype(jnp.int32)[None], rows.reshape(4, 4, 16, 1536))

    keep, send = pl.pallas_call(
        weight_kernel,
        grid=(6,),
        out_shape=(jax.ShapeDtypeStruct((2, 192, 3072), F32),) * 2,
        in_specs=[
            SMEM,
            SMEM,
            pl.BlockSpec((4, 8, 4, 16, 192), lambda i: (0, 0, 0, 0, 0)),
            pl.BlockSpec((512, 512), lambda i: (0, i)),
        ],
        out_specs=(pl.BlockSpec((2, 192, 512), lambda i: (0, 0, i)),) * 2,
        scratch_shapes=[pltpu.VMEM((768, 512), BF16)],
        compiler_params=LIMIT,
        cost_estimate=pl.CostEstimate(
            flops=2 * 512 * 3072 * 768, bytes_accessed=14 << 20, transcendentals=0
        ),
        name="weight_sums",
    )(owner, dest, cols, whole)
    met = swap(send, "core")
    passed = swap((keep[1] + met[1]).astype(BF16), "yl")
    grad_weight = (keep[0] + met[0] + passed.astype(F32)).astype(BF16)
    return grad_in, grad_weight


def solution(mesh):
    names = ("gx", "x", "zh", "yp", "yl", "core")
    fine = Mesh(mesh.devices.reshape(8, 4, 2, 2, 2, 2), names)
    split = P(("gx", "yp", "yl", "core"), ("x", "zh"))
    tokens = P("gx", ("yp", "yl", "core"))
    rows = P(("yp", "yl", "core", "gx"), ("x", "zh"))
    return jax.shard_map(
        shards,
        mesh=fine,
        in_specs=(tokens, rows, split, split),
        out_specs=(tokens, rows),
        check_vma=False,
    )
```

```python
import functools

import jax
import jax.numpy as jnp
from jax import lax
from jax.experimental import pallas as pl
from jax.experimental.pallas import tpu as pltpu
from jax.sharding import Mesh
from jax.sharding import PartitionSpec as P

RING = (0, 2, 4, 6, 7, 5, 3, 1)
STEPS = (0, -1, 1, -2, 2, -3, 3, 4)
F32 = jnp.float32
BF16 = jnp.bfloat16
VMEM = pl.BlockSpec(memory_space=pltpu.VMEM)
LIMIT = pltpu.CompilerParams(vmem_limit_bytes=48 * 1024 * 1024)
TILE = 768


def gelu_slope(value):
    scale = 0.7978845608028654
    tangent = jnp.tanh(scale * (value + 0.044715 * value * value * value))
    inner = scale * (1.0 + 3.0 * 0.044715 * value * value)
    return 0.5 * (1.0 + tangent) + 0.5 * value * (1.0 - tangent * tangent) * inner


def hop(value, step):
    return lax.ppermute(value, "gx", [(RING[q], RING[(q + step) % 8]) for q in range(8)])


def swap(value, axis):
    return lax.ppermute(value, axis, [(0, 1), (1, 0)])


def across(value):
    return lax.ppermute(value, ("yp", "yl"), [(k, 3 - k) for k in range(4)])


def owners():
    gx = lax.axis_index("gx")
    place = jnp.where(lax.rem(gx, 2) == 0, gx // 2, 7 - gx // 2)
    found = []
    for step in STEPS:
        q = lax.rem(place + step + 8, 8)
        found.append(jnp.where(q < 4, 2 * q, 15 - 2 * q))
    return found


def dests():
    yl, core = lax.axis_index("yl"), lax.axis_index("core")
    return [a * 2 + b for b in (core, 1 - core) for a in (yl, 1 - yl)]


def part_kernel(inputs, out):
    xp, xl, yp = (lax.axis_index(a) for a in ("xp", "xl", "yp"))
    for a in range(2):
        for c in range(2):
            y = jnp.where(xp == 0, yp * 2 + a, 3 - yp * 2 - a)
            block = inputs[pl.ds(pl.multiple_of(y * 64 + c * 32 + xl * 16, 16), 16)]
            for k in range(8):
                out[k * 4 + a * 2 + c] = block[:, k * 192 : (k + 1) * 192]


def product_kernel(*refs):
    pieces, weights, (rows, whole) = refs[:12], refs[12:16], refs[16:]
    owner, dest = owners(), dests()
    at = 0
    for piece in pieces:
        whole[at : at + piece.shape[0]] = piece[...]
        at += piece.shape[0]
    for j, weight in enumerate(weights):
        block = lax.dot_general(
            whole[...], weight[...], (((1,), (1,)), ((), ())), preferred_element_type=F32
        ).astype(BF16)
        for first in range(0, 512, 16):
            side, slot, half = first // 256, first // 32 % 8, first // 16 % 2
            rows[side * 2 + half, dest[j], owner[slot]] = block[first : first + 16]


def weight_kernel(j0, *refs):
    cols, (whole, out, held, turned) = refs[:3], refs[3:]

    @pl.when(pl.program_id(0) == 0)
    def _():
        own_x = lax.axis_index("xp") * 2 + lax.axis_index("xl")
        owner, dest = owners(), dests()
        held[own_x] = cols[0][...]
        held[own_x ^ 1] = cols[1][...]
        held[own_x ^ 2] = cols[2][0]
        held[own_x ^ 3] = cols[2][1]
        for j in range(2):
            parts = [
                held[side * 2 + half, owner[slot], dest[j0 + j]]
                for side in range(2)
                for slot in range(8)
                for half in range(2)
            ]
            turned[j * 192 : (j + 1) * 192] = jnp.concatenate(parts, 0).T

    total = jnp.dot(turned[...], whole[...], preferred_element_type=F32)
    for j in range(2):
        out[j] = total[j * 192 : (j + 1) * 192].astype(out.dtype)


def weight_sums(j0, dtype, cols, whole):
    part = pl.BlockSpec((8, 4, 16, 192), lambda i: (0, 0, 0, 0))
    return pl.pallas_call(
        functools.partial(weight_kernel, j0),
        grid=(3072 // TILE,),
        out_shape=jax.ShapeDtypeStruct((2, 192, 3072), dtype),
        in_specs=[part, part, pl.BlockSpec((2, 8, 4, 16, 192), lambda i: (0, 0, 0, 0, 0))]
        + [pl.BlockSpec((512, TILE), lambda i: (0, i))],
        out_specs=pl.BlockSpec((2, 192, TILE), lambda i: (0, 0, i)),
        scratch_shapes=[pltpu.VMEM((4, 8, 4, 16, 192), BF16), pltpu.VMEM((384, 512), BF16)],
        compiler_params=LIMIT,
        cost_estimate=pl.CostEstimate(
            flops=512 * 3072 * 768, bytes_accessed=8 << 20, transcendentals=0
        ),
        name="weight_sums",
    )(*cols, whole)


def add_kernel(parts, out):
    for k in range(8):
        for j in range(4):
            total = parts[0, j, k].astype(F32)
            for i in range(1, 4):
                total = total + parts[i, j, k].astype(F32)
            total = total.astype(BF16)
            out[k, 0, j] = total
            out[k, 1, j] = total


def pair_kernel(parts, out):
    sums = [parts[k, 0].astype(F32) + parts[k, 1].astype(F32) for k in range(8)]
    out[...] = jnp.concatenate(sums, 1).astype(BF16)


def place_kernel(parts, out):
    mine = lax.axis_index("yp")
    for p in range(2):
        side = jnp.where(mine == p, 0, 1)
        for s in range(2):
            source = jnp.where(mine == p, s, 1 - s)
            for c in range(2):
                for half in range(2):
                    first = p * 128 + s * 64 + c * 32 + half * 16
                    out[first : first + 16] = parts[side * 2 + half, source * 2 + c]


def meet_kernel(keep, met, own, passed):
    own[...] = keep[0] + met[0].astype(F32)
    passed[...] = (keep[1] + met[1].astype(F32)).astype(BF16)


def close_kernel(own, passed, out):
    out[...] = (own[...] + passed[...].astype(F32)).astype(BF16)


def whole_call(kernel, shape, name):
    return pl.pallas_call(
        kernel,
        out_shape=jax.ShapeDtypeStruct(shape, BF16),
        in_specs=[VMEM],
        out_specs=VMEM,
        compiler_params=LIMIT,
        name=name,
    )


def shards(inputs, weight, grad_out, pre_act):
    gh = (grad_out.astype(F32) * gelu_slope(pre_act.astype(F32))).astype(BF16)

    part = whole_call(part_kernel, (32, 16, 192), "part")(inputs)
    part, gh = lax.optimization_barrier((part, gh))
    part = lax.all_to_all(part, ("gx", "yl", "core"), split_axis=0, concat_axis=0, tiled=True)
    part = part.reshape(8, 4, 16, 192)

    up, down, far = [gh], [gh], []
    for s in range(3):
        up.append(hop(up[-1], 1))
        far.append(across(jnp.concatenate([down[-1], up[-1]], 0)))
        down.append(hop(down[-1], -1))
        if s == 0:
            up[1], down[1], part = lax.optimization_barrier((up[1], down[1], part))
            beside_x = swap(part, "xl")
        if s == 1:
            up[2], down[2], far[0] = lax.optimization_barrier((up[2], down[2], far[0]))
        if s == 2:
            up[3], down[3], far[1], beside_x = lax.optimization_barrier(
                (up[3], down[3], far[1], beside_x)
            )
            cols = (part, beside_x, swap(jnp.stack([part, beside_x], 0), "xp"))
    up.append(hop(up[3], 1))
    far.append(across(jnp.concatenate([down[3], up[4]], 0)))

    beside = swap(weight, "yl")
    weight, beside, up[2] = lax.optimization_barrier((weight, beside, up[2]))
    weights = (weight, beside, swap(weight, "core"), swap(beside, "core"))

    rows, whole = pl.pallas_call(
        product_kernel,
        out_shape=(
            jax.ShapeDtypeStruct((4, 4, 8, 16, 192), BF16),
            jax.ShapeDtypeStruct((512, 3072), BF16),
        ),
        in_specs=[VMEM] * 16,
        out_specs=(VMEM,) * 2,
        compiler_params=LIMIT,
        cost_estimate=pl.CostEstimate(
            flops=2 * 512 * 3072 * 768, bytes_accessed=12 << 20, transcendentals=0
        ),
        name="products",
    )(gh, up[1], down[1], up[2], down[2], up[3], down[3], up[4], *far, *weights)

    send = weight_sums(2, BF16, cols, whole)

    rows = lax.all_to_all(
        rows.reshape(16, 8, 16, 192),
        ("xp", "xl", "yl", "core"),
        split_axis=0,
        concat_axis=0,
        tiled=True,
    )
    rows, whole = lax.optimization_barrier((rows, whole))
    keep = weight_sums(0, F32, cols, whole)
    rows = whole_call(add_kernel, (8, 2, 4, 16, 192), "sum_x")(rows.reshape(4, 4, 8, 16, 192))
    rows = lax.all_to_all(
        rows.reshape(16, 64, 192), ("gx", "zh"), split_axis=0, concat_axis=0, tiled=True
    )
    rows = whole_call(pair_kernel, (64, 1536), "sum_z")(rows.reshape(8, 2, 64, 192))
    rows = lax.all_gather(rows, ("xp", "xl"), axis=0)
    grad_in = whole_call(place_kernel, (256, 1536), "place")(rows.reshape(4, 4, 16, 1536))

    met = swap(send, "core")
    pair = pl.BlockSpec((2, 192, TILE), lambda i: (0, 0, i))
    one = pl.BlockSpec((192, TILE), lambda i: (0, i))
    own, passed = pl.pallas_call(
        meet_kernel,
        grid=(3072 // TILE,),
        out_shape=(
            jax.ShapeDtypeStruct((192, 3072), F32),
            jax.ShapeDtypeStruct((192, 3072), BF16),
        ),
        in_specs=[pair, pair],
        out_specs=(one, one),
        compiler_params=LIMIT,
        name="meet",
    )(keep, met)
    grad_weight = pl.pallas_call(
        close_kernel,
        grid=(3072 // TILE,),
        out_shape=jax.ShapeDtypeStruct((192, 3072), BF16),
        in_specs=[one, one],
        out_specs=one,
        compiler_params=LIMIT,
        name="close",
    )(own, swap(passed, "yl"))
    return grad_in, grad_weight


def solution(mesh):
    names = ("gx", "xp", "xl", "zh", "yp", "yl", "core")
    fine = Mesh(mesh.devices.reshape(8, 2, 2, 2, 2, 2, 2), names)
    split = P(("gx", "yp", "yl", "core"), ("xp", "xl", "zh"))
    tokens = P("gx", ("yp", "yl", "core"))
    rows = P(("yp", "yl", "core", "gx"), ("xp", "xl", "zh"))
    return jax.shard_map(
        shards,
        mesh=fine,
        in_specs=(tokens, rows, split, split),
        out_specs=(tokens, rows),
        check_vma=False,
    )
```

```python
import functools

import jax
import jax.numpy as jnp
from jax import lax
from jax.experimental import pallas as pl
from jax.experimental.pallas import tpu as pltpu
from jax.sharding import Mesh
from jax.sharding import PartitionSpec as P

RING = (0, 2, 4, 6, 7, 5, 3, 1)
STEPS = (0, -1, 1, -2, 2, -3, 3, 4)
F32 = jnp.float32
BF16 = jnp.bfloat16
VMEM = pl.BlockSpec(memory_space=pltpu.VMEM)
LIMIT = pltpu.CompilerParams(vmem_limit_bytes=48 * 1024 * 1024)
TILE = 768


def gelu_slope(value):
    scale = 0.7978845608028654
    tangent = jnp.tanh(scale * (value + 0.044715 * value * value * value))
    inner = scale * (1.0 + 3.0 * 0.044715 * value * value)
    return 0.5 * (1.0 + tangent) + 0.5 * value * (1.0 - tangent * tangent) * inner


def hop(value, step):
    return lax.ppermute(value, "gx", [(RING[q], RING[(q + step) % 8]) for q in range(8)])


def swap(value, axis):
    return lax.ppermute(value, axis, [(0, 1), (1, 0)])


def across(value):
    return lax.ppermute(value, ("yp", "yl"), [(k, 3 - k) for k in range(4)])


def owners():
    gx = lax.axis_index("gx")
    place = jnp.where(lax.rem(gx, 2) == 0, gx // 2, 7 - gx // 2)
    found = []
    for step in STEPS:
        q = lax.rem(place + step + 8, 8)
        found.append(jnp.where(q < 4, 2 * q, 15 - 2 * q))
    return found


def dests():
    yl, core = lax.axis_index("yl"), lax.axis_index("core")
    return [a * 2 + b for b in (core, 1 - core) for a in (yl, 1 - yl)]


def part_kernel(inputs, out):
    xp, xl, yp = (lax.axis_index(a) for a in ("xp", "xl", "yp"))
    for a in range(2):
        for c in range(2):
            y = jnp.where(xp == 0, yp * 2 + a, 3 - yp * 2 - a)
            block = inputs[pl.ds(pl.multiple_of(y * 64 + c * 32 + xl * 16, 16), 16)]
            for k in range(8):
                out[k * 4 + a * 2 + c] = block[:, k * 192 : (k + 1) * 192]


def product_kernel(*refs):
    pieces, weights, (rows, whole) = refs[:12], refs[12:16], refs[16:]
    owner, dest = owners(), dests()
    at = 0
    for piece in pieces:
        whole[at : at + piece.shape[0]] = piece[...]
        at += piece.shape[0]
    for j, weight in enumerate(weights):
        block = lax.dot_general(
            whole[...], weight[...], (((1,), (1,)), ((), ())), preferred_element_type=F32
        ).astype(BF16)
        for first in range(0, 512, 16):
            side, slot, half = first // 256, first // 32 % 8, first // 16 % 2
            rows[side * 2 + half, dest[j], owner[slot]] = block[first : first + 16]


def weight_kernel(j0, *refs):
    cols, (whole, out, held, turned) = refs[:3], refs[3:]

    @pl.when(pl.program_id(0) == 0)
    def _():
        own_x = lax.axis_index("xp") * 2 + lax.axis_index("xl")
        owner, dest = owners(), dests()
        held[own_x] = cols[0][...]
        held[own_x ^ 1] = cols[1][...]
        held[own_x ^ 2] = cols[2][0]
        held[own_x ^ 3] = cols[2][1]
        for j in range(2):
            parts = [
                held[side * 2 + half, owner[slot], dest[j0 + j]]
                for side in range(2)
                for slot in range(8)
                for half in range(2)
            ]
            turned[j * 192 : (j + 1) * 192] = jnp.concatenate(parts, 0).T

    total = jnp.dot(turned[...], whole[...], preferred_element_type=F32)
    for j in range(2):
        out[j] = total[j * 192 : (j + 1) * 192].astype(out.dtype)


def weight_sums(j0, dtype, cols, whole):
    part = pl.BlockSpec((8, 4, 16, 192), lambda i: (0, 0, 0, 0))
    return pl.pallas_call(
        functools.partial(weight_kernel, j0),
        grid=(3072 // TILE,),
        out_shape=jax.ShapeDtypeStruct((2, 192, 3072), dtype),
        in_specs=[part, part, pl.BlockSpec((2, 8, 4, 16, 192), lambda i: (0, 0, 0, 0, 0))]
        + [pl.BlockSpec((512, TILE), lambda i: (0, i))],
        out_specs=pl.BlockSpec((2, 192, TILE), lambda i: (0, 0, i)),
        scratch_shapes=[pltpu.VMEM((4, 8, 4, 16, 192), BF16), pltpu.VMEM((384, 512), BF16)],
        compiler_params=LIMIT,
        cost_estimate=pl.CostEstimate(
            flops=512 * 3072 * 768, bytes_accessed=8 << 20, transcendentals=0
        ),
        name="weight_sums",
    )(*cols, whole)


def add_kernel(parts, out):
    for k in range(8):
        for j in range(4):
            total = parts[0, j, k].astype(F32)
            for i in range(1, 4):
                total = total + parts[i, j, k].astype(F32)
            total = total.astype(BF16)
            out[k, 0, j] = total
            out[k, 1, j] = total


def pair_kernel(parts, out):
    sums = [parts[k, 0].astype(F32) + parts[k, 1].astype(F32) for k in range(8)]
    total = jnp.concatenate(sums, 1).astype(BF16)
    for x in range(4):
        out[x] = total


def place_kernel(parts, out):
    mine = lax.axis_index("yp")
    for p in range(2):
        side = jnp.where(mine == p, 0, 1)
        for s in range(2):
            source = jnp.where(mine == p, s, 1 - s)
            for c in range(2):
                for half in range(2):
                    first = p * 128 + s * 64 + c * 32 + half * 16
                    out[first : first + 16] = parts[side * 2 + half, source * 2 + c]


def meet_kernel(keep, met, own, passed):
    own[...] = keep[0] + met[0].astype(F32)
    passed[...] = (keep[1] + met[1].astype(F32)).astype(BF16)


def close_kernel(own, passed, out):
    out[...] = (own[...] + passed[...].astype(F32)).astype(BF16)


def whole_call(kernel, shape, name):
    return pl.pallas_call(
        kernel,
        out_shape=jax.ShapeDtypeStruct(shape, BF16),
        in_specs=[VMEM],
        out_specs=VMEM,
        compiler_params=LIMIT,
        name=name,
    )


def shards(inputs, weight, grad_out, pre_act):
    gh = (grad_out.astype(F32) * gelu_slope(pre_act.astype(F32))).astype(BF16)

    part = whole_call(part_kernel, (32, 16, 192), "part")(inputs)
    part, gh = lax.optimization_barrier((part, gh))
    part = lax.all_to_all(part, ("gx", "yl", "core"), split_axis=0, concat_axis=0, tiled=True)
    part = part.reshape(8, 4, 16, 192)

    up, down, far = [gh], [gh], []
    for s in range(3):
        up.append(hop(up[-1], 1))
        far.append(across(jnp.concatenate([down[-1], up[-1]], 0)))
        down.append(hop(down[-1], -1))
        if s == 1:
            up[2], down[2], far[0] = lax.optimization_barrier((up[2], down[2], far[0]))
        if s == 2:
            up[3], down[3], far[1], part = lax.optimization_barrier((up[3], down[3], far[1], part))
            beside_x = swap(part, "xl")
            cols = (part, beside_x, swap(jnp.stack([part, beside_x], 0), "xp"))
    up.append(hop(up[3], 1))
    far.append(across(jnp.concatenate([down[3], up[4]], 0)))

    beside = swap(weight, "yl")
    weight, beside, up[2] = lax.optimization_barrier((weight, beside, up[2]))
    weights = (weight, beside, swap(weight, "core"), swap(beside, "core"))

    rows, whole = pl.pallas_call(
        product_kernel,
        out_shape=(
            jax.ShapeDtypeStruct((4, 4, 8, 16, 192), BF16),
            jax.ShapeDtypeStruct((512, 3072), BF16),
        ),
        in_specs=[VMEM] * 16,
        out_specs=(VMEM,) * 2,
        compiler_params=LIMIT,
        cost_estimate=pl.CostEstimate(
            flops=2 * 512 * 3072 * 768, bytes_accessed=12 << 20, transcendentals=0
        ),
        name="products",
    )(gh, up[1], down[1], up[2], down[2], up[3], down[3], up[4], *far, *weights)

    send = weight_sums(2, BF16, cols, whole)

    rows = lax.all_to_all(
        rows.reshape(16, 8, 16, 192),
        ("xp", "xl", "yl", "core"),
        split_axis=0,
        concat_axis=0,
        tiled=True,
    )
    rows, whole = lax.optimization_barrier((rows, whole))
    keep = weight_sums(0, F32, cols, whole)
    rows = whole_call(add_kernel, (8, 2, 4, 16, 192), "sum_x")(rows.reshape(4, 4, 8, 16, 192))
    rows = lax.all_to_all(
        rows.reshape(16, 64, 192), ("gx", "zh"), split_axis=0, concat_axis=0, tiled=True
    )
    rows = whole_call(pair_kernel, (4, 64, 1536), "sum_z")(rows.reshape(8, 2, 64, 192))
    rows = lax.all_to_all(rows, ("xp", "xl"), split_axis=0, concat_axis=0, tiled=True)
    grad_in = whole_call(place_kernel, (256, 1536), "place")(rows.reshape(4, 4, 16, 1536))

    met = swap(send, "core")
    pair = pl.BlockSpec((2, 192, TILE), lambda i: (0, 0, i))
    one = pl.BlockSpec((192, TILE), lambda i: (0, i))
    own, passed = pl.pallas_call(
        meet_kernel,
        grid=(3072 // TILE,),
        out_shape=(
            jax.ShapeDtypeStruct((192, 3072), F32),
            jax.ShapeDtypeStruct((192, 3072), BF16),
        ),
        in_specs=[pair, pair],
        out_specs=(one, one),
        compiler_params=LIMIT,
        name="meet",
    )(keep, met)
    grad_weight = pl.pallas_call(
        close_kernel,
        grid=(3072 // TILE,),
        out_shape=jax.ShapeDtypeStruct((192, 3072), BF16),
        in_specs=[one, one],
        out_specs=one,
        compiler_params=LIMIT,
        name="close",
    )(own, swap(passed, "yl"))
    return grad_in, grad_weight


def solution(mesh):
    names = ("gx", "xp", "xl", "zh", "yp", "yl", "core")
    fine = Mesh(mesh.devices.reshape(8, 2, 2, 2, 2, 2, 2), names)
    split = P(("gx", "yp", "yl", "core"), ("xp", "xl", "zh"))
    tokens = P("gx", ("yp", "yl", "core"))
    rows = P(("yp", "yl", "core", "gx"), ("xp", "xl", "zh"))
    return jax.shard_map(
        shards,
        mesh=fine,
        in_specs=(tokens, rows, split, split),
        out_specs=(tokens, rows),
        check_vma=False,
    )
```

```python
import functools

import jax
import jax.numpy as jnp
from jax import lax
from jax.experimental import pallas as pl
from jax.experimental.pallas import tpu as pltpu
from jax.sharding import Mesh
from jax.sharding import PartitionSpec as P

RING = (0, 2, 4, 6, 7, 5, 3, 1)
STEPS = (0, -1, 1, -2, 2, -3, 3, 4)
F32 = jnp.float32
BF16 = jnp.bfloat16
VMEM = pl.BlockSpec(memory_space=pltpu.VMEM)
LIMIT = pltpu.CompilerParams(vmem_limit_bytes=48 * 1024 * 1024)
TILE = 768


def gelu_slope(value):
    scale = 0.7978845608028654
    tangent = jnp.tanh(scale * (value + 0.044715 * value * value * value))
    inner = scale * (1.0 + 3.0 * 0.044715 * value * value)
    return 0.5 * (1.0 + tangent) + 0.5 * value * (1.0 - tangent * tangent) * inner


def hop(value, step):
    return lax.ppermute(value, "gx", [(RING[q], RING[(q + step) % 8]) for q in range(8)])


def swap(value, axis):
    return lax.ppermute(value, axis, [(0, 1), (1, 0)])


def across(value):
    return lax.ppermute(value, ("yp", "yl"), [(k, 3 - k) for k in range(4)])


def owners():
    gx = lax.axis_index("gx")
    place = jnp.where(lax.rem(gx, 2) == 0, gx // 2, 7 - gx // 2)
    found = []
    for step in STEPS:
        q = lax.rem(place + step + 8, 8)
        found.append(jnp.where(q < 4, 2 * q, 15 - 2 * q))
    return found


def dests():
    yl, core = lax.axis_index("yl"), lax.axis_index("core")
    return [a * 2 + b for b in (core, 1 - core) for a in (yl, 1 - yl)]


def part_kernel(inputs, out):
    xp, xl, yp = (lax.axis_index(a) for a in ("xp", "xl", "yp"))
    for a in range(2):
        for c in range(2):
            y = jnp.where(xp == 0, yp * 2 + a, 3 - yp * 2 - a)
            block = inputs[pl.ds(pl.multiple_of(y * 64 + c * 32 + xl * 16, 16), 16)]
            for k in range(8):
                out[k * 4 + a * 2 + c] = block[:, k * 192 : (k + 1) * 192]


def product_kernel(*refs):
    pieces, weights, (rows, whole) = refs[:12], refs[12:16], refs[16:]
    owner, dest = owners(), dests()
    at = 0
    for piece in pieces:
        whole[at : at + piece.shape[0]] = piece[...]
        at += piece.shape[0]
    for j, weight in enumerate(weights):
        block = lax.dot_general(
            whole[...], weight[...], (((1,), (1,)), ((), ())), preferred_element_type=F32
        ).astype(BF16)
        for first in range(0, 512, 16):
            side, slot, half = first // 256, first // 32 % 8, first // 16 % 2
            rows[side * 2 + half, dest[j], owner[slot]] = block[first : first + 16]


def weight_kernel(j0, *refs):
    cols, (whole, out, held, turned) = refs[:3], refs[3:]

    @pl.when(pl.program_id(0) == 0)
    def _():
        own_x = lax.axis_index("xp") * 2 + lax.axis_index("xl")
        owner, dest = owners(), dests()
        held[own_x] = cols[0][...]
        held[own_x ^ 1] = cols[1][...]
        held[own_x ^ 2] = cols[2][0]
        held[own_x ^ 3] = cols[2][1]
        for j in range(2):
            parts = [
                held[side * 2 + half, owner[slot], dest[j0 + j]]
                for side in range(2)
                for slot in range(8)
                for half in range(2)
            ]
            turned[j * 192 : (j + 1) * 192] = jnp.concatenate(parts, 0).T

    total = jnp.dot(turned[...], whole[...], preferred_element_type=F32)
    for j in range(2):
        out[j] = total[j * 192 : (j + 1) * 192].astype(out.dtype)


def weight_sums(j0, dtype, cols, whole):
    part = pl.BlockSpec((8, 4, 16, 192), lambda i: (0, 0, 0, 0))
    return pl.pallas_call(
        functools.partial(weight_kernel, j0),
        grid=(3072 // TILE,),
        out_shape=jax.ShapeDtypeStruct((2, 192, 3072), dtype),
        in_specs=[part, part, pl.BlockSpec((2, 8, 4, 16, 192), lambda i: (0, 0, 0, 0, 0))]
        + [pl.BlockSpec((512, TILE), lambda i: (0, i))],
        out_specs=pl.BlockSpec((2, 192, TILE), lambda i: (0, 0, i)),
        scratch_shapes=[pltpu.VMEM((4, 8, 4, 16, 192), BF16), pltpu.VMEM((384, 512), BF16)],
        compiler_params=LIMIT,
        cost_estimate=pl.CostEstimate(
            flops=512 * 3072 * 768, bytes_accessed=8 << 20, transcendentals=0
        ),
        name="weight_sums",
    )(*cols, whole)


def add_kernel(parts, out):
    for k in range(8):
        for j in range(4):
            total = parts[0, j, k].astype(F32)
            for i in range(1, 4):
                total = total + parts[i, j, k].astype(F32)
            total = total.astype(BF16)
            out[k, 0, j] = total
            out[k, 1, j] = total


def pair_kernel(parts, out):
    sums = [parts[k, 0].astype(F32) + parts[k, 1].astype(F32) for k in range(8)]
    total = jnp.concatenate(sums, 1).astype(BF16)
    for x in range(4):
        out[x] = total


def place_kernel(parts, out):
    mine = lax.axis_index("yp")
    for p in range(2):
        side = jnp.where(mine == p, 0, 1)
        for s in range(2):
            source = jnp.where(mine == p, s, 1 - s)
            for c in range(2):
                for half in range(2):
                    first = p * 128 + s * 64 + c * 32 + half * 16
                    out[first : first + 16] = parts[side * 2 + half, source * 2 + c]


def meet_kernel(keep, met, own, passed):
    own[...] = keep[0] + met[0].astype(F32)
    passed[...] = (keep[1] + met[1].astype(F32)).astype(BF16)


def close_kernel(own, passed, out):
    out[...] = (own[...] + passed[...].astype(F32)).astype(BF16)


def whole_call(kernel, shape, name):
    return pl.pallas_call(
        kernel,
        out_shape=jax.ShapeDtypeStruct(shape, BF16),
        in_specs=[VMEM],
        out_specs=VMEM,
        compiler_params=LIMIT,
        name=name,
    )


def shards(inputs, weight, grad_out, pre_act):
    gh = (grad_out.astype(F32) * gelu_slope(pre_act.astype(F32))).astype(BF16)

    part = whole_call(part_kernel, (32, 16, 192), "part")(inputs)
    part = lax.all_to_all(part, ("gx", "yl", "core"), split_axis=0, concat_axis=0, tiled=True)
    part = part.reshape(8, 4, 16, 192)

    up, down, far = [gh], [gh], []
    for s in range(3):
        up.append(hop(up[-1], 1))
        far.append(across(jnp.concatenate([down[-1], up[-1]], 0)))
        down.append(hop(down[-1], -1))
        if s == 1:
            up[2], down[2] = lax.optimization_barrier((up[2], down[2]))
        if s == 2:
            up[3], down[3], far[1], part = lax.optimization_barrier((up[3], down[3], far[1], part))
            beside_x = swap(part, "xl")
            cols = (part, beside_x, swap(jnp.stack([part, beside_x], 0), "xp"))
    up.append(hop(up[3], 1))
    far.append(across(jnp.concatenate([down[3], up[4]], 0)))

    beside = swap(weight, "yl")
    weight, beside, up[2] = lax.optimization_barrier((weight, beside, up[2]))
    weights = (weight, beside, swap(weight, "core"), swap(beside, "core"))

    rows, whole = pl.pallas_call(
        product_kernel,
        out_shape=(
            jax.ShapeDtypeStruct((4, 4, 8, 16, 192), BF16),
            jax.ShapeDtypeStruct((512, 3072), BF16),
        ),
        in_specs=[VMEM] * 16,
        out_specs=(VMEM,) * 2,
        compiler_params=LIMIT,
        cost_estimate=pl.CostEstimate(
            flops=2 * 512 * 3072 * 768, bytes_accessed=12 << 20, transcendentals=0
        ),
        name="products",
    )(gh, up[1], down[1], up[2], down[2], up[3], down[3], up[4], *far, *weights)

    send = weight_sums(2, BF16, cols, whole)

    rows = lax.all_to_all(
        rows.reshape(16, 8, 16, 192),
        ("xp", "xl", "yl", "core"),
        split_axis=0,
        concat_axis=0,
        tiled=True,
    )
    rows, whole = lax.optimization_barrier((rows, whole))
    keep = weight_sums(0, F32, cols, whole)
    rows = whole_call(add_kernel, (8, 2, 4, 16, 192), "sum_x")(rows.reshape(4, 4, 8, 16, 192))
    rows = lax.all_to_all(
        rows.reshape(16, 64, 192), ("gx", "zh"), split_axis=0, concat_axis=0, tiled=True
    )
    rows = whole_call(pair_kernel, (4, 64, 1536), "sum_z")(rows.reshape(8, 2, 64, 192))
    rows = lax.all_to_all(rows, ("xp", "xl"), split_axis=0, concat_axis=0, tiled=True)
    grad_in = whole_call(place_kernel, (256, 1536), "place")(rows.reshape(4, 4, 16, 1536))

    met = swap(send, "core")
    pair = pl.BlockSpec((2, 192, TILE), lambda i: (0, 0, i))
    one = pl.BlockSpec((192, TILE), lambda i: (0, i))
    own, passed = pl.pallas_call(
        meet_kernel,
        grid=(3072 // TILE,),
        out_shape=(
            jax.ShapeDtypeStruct((192, 3072), F32),
            jax.ShapeDtypeStruct((192, 3072), BF16),
        ),
        in_specs=[pair, pair],
        out_specs=(one, one),
        compiler_params=LIMIT,
        name="meet",
    )(keep, met)
    grad_weight = pl.pallas_call(
        close_kernel,
        grid=(3072 // TILE,),
        out_shape=jax.ShapeDtypeStruct((192, 3072), BF16),
        in_specs=[one, one],
        out_specs=one,
        compiler_params=LIMIT,
        name="close",
    )(own, swap(passed, "yl"))
    return grad_in, grad_weight


def solution(mesh):
    names = ("gx", "xp", "xl", "zh", "yp", "yl", "core")
    fine = Mesh(mesh.devices.reshape(8, 2, 2, 2, 2, 2, 2), names)
    split = P(("gx", "yp", "yl", "core"), ("xp", "xl", "zh"))
    tokens = P("gx", ("yp", "yl", "core"))
    rows = P(("yp", "yl", "core", "gx"), ("xp", "xl", "zh"))
    return jax.shard_map(
        shards,
        mesh=fine,
        in_specs=(tokens, rows, split, split),
        out_specs=(tokens, rows),
        check_vma=False,
    )
```
